32 devices in a mesh: vc: 4 (over z), vd: 8 (over y, x, core).
Axes of the slice: x: 2, y: 2, z: 4, core: 2. Of those that a mesh axis runs over, the one named last changes fastest.
Arguments:
- vectors_left: float32 [8, 1024, 4096], P(None, 'vc', 'vd'), may hold values from -0.8 to 0.8
- vectors_right: float32 [16, 1024, 4096], P(None, 'vd', 'vc'), may hold values from -0.8 to 0.8
- amplitudes: float32 [1024, 1024, 128], P('vc', 'vd'), may hold values from -0.005859375 to 0.005859375
Outputs:
- ladder: float32 [128, 8, 16], P('vd', None, 'vc')
The draws below stay inside these ranges and needn't reach their ends.
All inputs are finite; a program needn't handle non-finite values.
Results may differ from the reference program's by a relative error of at most 0.000094.
Values sent between devices are 32-bit elements; how exact they have to be, the bound alone decides.
A program may use at most 192 MiB of HBM per device.

```python
import jax
import jax.numpy as jnp
from jax import lax

NV = 1024
NQ = 4096
NIJ = 128
NA = 8
NB = 16


def block_levels(rng, dims, shards, low, largest):
    def one(dim, parts):
        draws = jax.random.uniform(jax.random.fold_in(jax.random.fold_in(rng, 6), dim), (parts,), jnp.float32, low / len(shards), largest / len(shards))
        return jnp.repeat(jnp.exp(draws), dims[dim] // parts).reshape((-1,) + (1,) * (len(dims) - dim - 1))

    loudness = one(*shards[0])
    for cut in shards[1:]:
        loudness = loudness * one(*cut)
    return loudness


def noise(own_key, shape, deviation, reach, pieces=(), dtype=jnp.bfloat16):
    loudness = block_levels(own_key, shape, pieces, -0.22, 0.18) if pieces else 1.0
    values = jax.random.normal(own_key, shape, jnp.float32) * deviation * loudness
    return jnp.minimum(jnp.maximum(values, -reach), reach).astype(dtype)


def setup_inputs(seed: int = 0) -> dict:
    key_list = jax.random.split(jax.random.key(seed), 4)
    vectors_left = noise(key_list[0], (NA, NV, NQ), 0.134, 0.8, ((1, 4), (2, 8)), jnp.float32)
    vectors_right = noise(key_list[1], (NB, NV, NQ), 0.134, 0.8, ((1, 8), (2, 4)), jnp.float32)
    amplitudes = noise(key_list[2], (NV, NV, NIJ), (NV * NV) ** -0.5, 0.005859375, ((0, 4), (1, 8)), jnp.float32)
    return dict(vectors_left=vectors_left, vectors_right=vectors_right, amplitudes=amplitudes)


def reference(vectors_left, vectors_right, amplitudes):
    left_flat = vectors_left.reshape(NA * NV, NQ)
    right_flat = vectors_right.reshape(NB * NV, NQ)
    integrals = lax.dot_general(left_flat, right_flat, (((1,), (1,)), ((), ())), precision=lax.Precision.HIGHEST, preferred_element_type=jnp.float32)
    integrals = integrals.reshape(NA, NV, NB, NV)
    return jnp.einsum("acbd,cdi->iab", integrals, amplitudes, precision=lax.Precision.HIGHEST)
```

```python
import functools

import jax
import jax.numpy as jnp
from jax import lax
from jax.experimental import pallas as pl
from jax.experimental.pallas import tpu as pltpu
from jax.sharding import PartitionSpec as P

MESH = pl.DeviceIdType.MESH
CHUNK = 256
AHEAD = 2


def contract(left_rows, right_rows):
    return lax.dot_general(
        left_rows,
        right_rows,
        (((1,), (1,)), ((), ())),
        precision=lax.Precision.HIGHEST,
        preferred_element_type=jnp.float32,
    )


def plain(vectors_left, vectors_right, amplitudes):
    count_a, count_c, left_q = vectors_left.shape
    count_b, count_d, right_q = vectors_right.shape
    left_whole = lax.all_gather(vectors_left, "vd", axis=2, tiled=True)
    left_flat = left_whole.reshape(count_a * count_c, left_whole.shape[2])
    piece = lax.all_gather(vectors_right, "vc", axis=2, tiled=True)
    width = piece.shape[2]
    tile = contract(left_flat, piece.reshape(count_b * count_d, width))
    tile = tile.reshape(count_a, count_c, count_b, count_d)
    partial_sum = jnp.einsum("acbd,cdi->iab", tile, amplitudes, precision=lax.Precision.HIGHEST)
    reduced = lax.psum_scatter(partial_sum, "vd", scatter_dimension=0, tiled=True)
    return lax.psum_scatter(reduced, "vc", scatter_dimension=2, tiled=True)


def split(x):
    hi = x.astype(jnp.bfloat16)
    lo = (x - hi.astype(jnp.float32)).astype(jnp.bfloat16)
    return hi, lo


def kernel(nz, nd, main, left, right, amps, out, lg, rg, te, acc, own_rest, far_rest,
           lbuf, rbuf, ls, rs, tbuf, total, red_d, red_c,
           z_send, z_recv, m_send, m_recv, e_send, e_recv, le_send, le_recv, te_send, te_recv,
           lg_send, lg_recv, d_send, d_recv, c_send, c_recv, local, tsem):
    count_a, count_c, left_q = left.shape
    count_d, count_b, right_q = right.shape
    rest = count_d - main
    per = right_q // CHUNK
    half = left_q // 2
    rows_main, rows_rest = main * count_b, rest * count_b
    i = lax.axis_index("vc")
    j = lax.axis_index("vd")
    core, x, y = j % 2, (j // 2) % 2, j // 4
    jx, jy, js = j + 2 - 4 * x, j + 4 - 8 * y, j + 1 - 2 * core
    jd = jx + 4 - 8 * y
    is_end = (i == 0) | (i == nz - 1)
    middle = jnp.logical_not(is_end)
    low = i < nz // 2
    partner = jnp.where(low, 1 - i, 2 * nz - 3 - i)
    across = nz - 1 - i

    barrier = pltpu.get_barrier_semaphore()
    for step in range(1, nd):
        pl.semaphore_signal(barrier, inc=1, device_id=(i, (j + step) % nd), device_id_type=MESH)
    for step in range(1, nz):
        pl.semaphore_signal(barrier, inc=1, device_id=((i + step) % nz, j), device_id_type=MESH)
    pl.semaphore_wait(barrier, nd - 1 + nz - 1)

    def remote(src, dst, send, recv, who):
        return pltpu.make_async_remote_copy(
            src_ref=src, dst_ref=dst, send_sem=send, recv_sem=recv, device_id=who, device_id_type=MESH)

    n_send = (jnp.where(i < nz - 1, per * (i + 1), 0), jnp.where(i > 0, per * (nz - i), 0))
    n_recv = (per * i, per * (nz - 1 - i))

    def z_copy(way, n, src_own):
        block = jnp.where(way == 0, i - n // per, i + n // per) if src_own is None else i
        cols = pl.ds(pl.multiple_of((n % per) * CHUNK, CHUNK), CHUNK)
        dst = rg.at[block, pl.ds(0, main), :, cols]
        src = right.at[pl.ds(0, main), :, cols] if src_own else dst
        who = (i + 1, j) if way == 0 else (i - 1, j)
        return remote(src, dst, z_send.at[way, n], z_recv.at[way, n], who)

    def z_start(way, n):
        @pl.when((n < per) & (n < n_send[way]))
        def _():
            z_copy(way, n, True).start()

        @pl.when((n >= per) & (n < n_send[way]))
        def _():
            z_copy(way, n, None).start()

    def z_wait_recv(way, n):
        block = i - 1 - n // per if way == 0 else i + 1 + n // per
        cols = pl.ds(pl.multiple_of((n % per) * CHUNK, CHUNK), CHUNK)
        dst = rg.at[block, pl.ds(0, main), :, cols]
        remote(dst, dst, z_send.at[way, n], z_recv.at[way, n], (partner, j)).wait_recv()

    def z_wait_send(way, n):
        cols = pl.ds(pl.multiple_of((n % per) * CHUNK, CHUNK), CHUNK)
        src = right.at[pl.ds(0, main), :, cols]
        remote(src, src, z_send.at[way, n], z_recv.at[way, n], (partner, j)).wait_send()

    def e_copy(k):
        cols = pl.ds(k * CHUNK, CHUNK)
        return remote(right.at[pl.ds(main, rest), :, cols], rg.at[i, pl.ds(main, rest), :, cols],
                      e_send.at[k], e_recv.at[k], (partner, j))

    def m_start(r):
        cols = pl.ds(pl.multiple_of((r % per) * CHUNK, CHUNK), CHUNK)

        @pl.when(r < per)
        def _():
            remote(right.at[pl.ds(main, rest), :, cols], rg.at[i, pl.ds(main, rest), :, cols],
                   m_send.at[r], m_recv.at[r], (across, j)).start()

        @pl.when((r >= per) & (r < 2 * per))
        def _():
            block = rg.at[partner, pl.ds(main, rest), :, cols]
            remote(block, block, m_send.at[r], m_recv.at[r], (across, j)).start()

    def m_copy(r):
        cols = pl.ds(pl.multiple_of((r % per) * CHUNK, CHUNK), CHUNK)
        block = jnp.where(r < per, across, nz - 1 - partner)
        ref = rg.at[block, pl.ds(main, rest), :, cols]
        return remote(ref, ref, m_send.at[r], m_recv.at[r], (across, j))

    def le_copy(h):
        cols = pl.ds(h * half, half)
        return remote(left.at[:, :, cols], lg.at[1, j, :, :, cols],
                      le_send.at[h], le_recv.at[h], (partner, j))

    def te_copy():
        return remote(amps.at[:, pl.ds(main, rest), :], te, te_send, te_recv, (partner, j))

    def lg_copy(g, n):
        h0, h1 = pl.ds(0, half), pl.ds(half, half)
        src, to = (
            (lg.at[g, j], jx), (lg.at[g, j], jy), (lg.at[g, j], js),
            (lg.at[g, jx, :, :, h0], jy), (lg.at[g, jy, :, :, h1], jx),
            (lg.at[g, jx], js), (lg.at[g, jy], js), (lg.at[g, jd], js),
        )[n]
        return remote(src, src, lg_send.at[g, n], lg_recv.at[g, n], (i, to))

    def lg_first(g):
        for n in (0, 1, 2):
            lg_copy(g, n).start()

    def lg_second(g):
        for n in (0, 1):
            lg_copy(g, n).wait_recv()
        for n in (3, 4, 5, 6):
            lg_copy(g, n).start()

    def lg_third(g):
        for n in (3, 4):
            lg_copy(g, n).wait_recv()
        lg_copy(g, 7).start()

    def lg_last(g):
        for n in (2, 5, 6, 7):
            lg_copy(g, n).wait_recv()

    def load_left(g, block, k):
        vec = block * right_q + k * CHUNK
        src = lg.at[g, vec // left_q, :, :, pl.ds(pl.multiple_of(vec % left_q, CHUNK), CHUNK)]
        return pltpu.make_async_copy(src, lbuf, local.at[0])

    def load_right(block, k, start, size):
        src = rg.at[block, pl.ds(start, size), :, pl.ds(pl.multiple_of(k * CHUNK, CHUNK), CHUNK)]
        return pltpu.make_async_copy(src, rbuf.at[pl.ds(0, size)], local.at[1])

    def split_left():
        @pl.loop(0, count_a)
        def _(a):
            hi, lo = split(lbuf[a])
            rows = pl.ds(pl.multiple_of(a * count_c, count_c), count_c)
            ls[rows, 0:CHUNK] = hi
            ls[rows, CHUNK:2 * CHUNK] = lo
            ls[rows, 2 * CHUNK:3 * CHUNK] = hi

    def split_right(size):
        @pl.loop(0, size // 8)
        def _(g):
            hi, lo = split(rbuf[pl.ds(g * 8, 8)].reshape(8 * count_b, CHUNK))
            rows = pl.ds(pl.multiple_of(g * 8 * count_b, 8 * count_b), 8 * count_b)
            rs[rows, 0:CHUNK] = hi
            rs[rows, CHUNK:2 * CHUNK] = hi
            rs[rows, 2 * CHUNK:3 * CHUNK] = lo

    def multiply(target, rows):
        parts = 2 if rows > 1024 else 1
        size = rows // parts

        @pl.loop(0, count_a)
        def _(a):
            cols = pl.ds(pl.multiple_of(a * count_c, count_c), count_c)
            for part in range(parts):
                span = pl.ds(part * size, size)
                target[span, cols] += lax.dot_general(
                    rs[span, :], ls[cols, :], (((1,), (1,)), ((), ())),
                    preferred_element_type=jnp.float32)

    def main_task(block, k):
        a, b = load_left(0, block, k), load_right(block, k, 0, main)
        a.start()
        b.start()
        a.wait()
        split_left()
        b.wait()
        split_right(main)
        multiply(acc, rows_main)

    def rest_task(block, k):
        b = load_right(block, k, main, rest)
        b.start()
        a = load_left(0, block, k)
        a.start()
        b.wait()
        split_right(rest)
        a.wait()
        split_left()
        a = load_left(1, block, k)
        a.start()
        multiply(own_rest, rows_rest)
        a.wait()
        split_left()
        multiply(far_rest, rows_rest)

    for way in (0, 1):
        for n in range(AHEAD):
            z_start(way, n)
    keep_left = pltpu.make_async_copy(left, lg.at[0, j], local.at[0])
    keep_right = pltpu.make_async_copy(right, rg.at[i], local.at[1])
    keep_left.start()
    keep_right.start()

    @pl.when(is_end)
    def _():
        for h in (0, 1):
            le_copy(h).start()

    keep_left.wait()
    lg_first(0)

    @pl.loop(0, count_a)
    def _(a):
        cols = pl.ds(pl.multiple_of(a * count_c, count_c), count_c)
        acc[:, cols] = jnp.zeros((rows_main, count_c), jnp.float32)
        own_rest[:, cols] = jnp.zeros((rows_rest, count_c), jnp.float32)
        far_rest[:, cols] = jnp.zeros((rows_rest, count_c), jnp.float32)

    keep_right.wait()

    steps = (nz - 1) * per

    def last_task(t):
        return jnp.where(t < 5, 0, jnp.minimum(jnp.minimum(per + 6 * (t - 5), per + 2 * (t + 1)), per + 2 * steps))

    @pl.loop(0, 15)
    def _(t):
        for way in (0, 1):
            @pl.when(t < n_recv[way])
            def _(way=way):
                z_wait_recv(way, t)

        for way in (0, 1):
            @pl.when(t + AHEAD < n_send[way])
            def _(way=way):
                z_wait_send(way, t)

            z_start(way, t + AHEAD)

        @pl.when(is_end)
        def _():
            @pl.when(t == 3)
            def _():
                for k in range(2):
                    e_copy(k).start()

            @pl.when(t == 4)
            def _():
                for k in range(2, per):
                    e_copy(k).start()

            @pl.when(t == 6)
            def _():
                te_copy().start()

        @pl.when(t == 2)
        def _():
            lg_second(0)

        @pl.when((t == 3) & middle)
        def _():
            for h in (0, 1):
                le_copy(h).wait_recv()
            lg_first(1)

        @pl.when(t == 4)
        def _():
            lg_third(0)

        @pl.when(t == 5)
        def _():
            lg_last(0)

        @pl.when(middle)
        def _():
            @pl.when(t == 5)
            def _():
                lg_second(1)

            @pl.when(t == 6)
            def _():
                for r in range(AHEAD):
                    m_start(r)

            @pl.when(t == 7)
            def _():
                lg_third(1)

            @pl.when(t == 8)
            def _():
                lg_last(1)

            @pl.when(t == 9)
            def _():
                for k in range(per):
                    e_copy(k).wait_recv()

            @pl.when(t >= 7)
            def _():
                m_copy(t - 7).wait_send()
                m_start(t - 7 + AHEAD)
                m_copy(t - 7).wait_recv()

        def do_main(q, carry):
            u, way = (q - per) // 2, (q - per) % 2
            own = q < per
            block = jnp.where(own, i, jnp.where(way == 0, i - 1 - u // per, i + 1 + u // per))
            k = jnp.where(own, q, u % per)

            @pl.when(own | (u < jnp.where(way == 0, n_recv[0], n_recv[1])))
            def _():
                main_task(block, k)

            return carry

        lax.fori_loop(last_task(t - 1), last_task(t), do_main, 0)

        def do_rest(p, carry):
            source = p // per
            block = jnp.where(source == 0, i, jnp.where(source == 1, partner, jnp.where(
                source == 2, across, nz - 1 - partner)))
            rest_task(block, p % per)
            return carry

        def last_rest(t):
            return jnp.where(t < 8, 0, jnp.where(t < 11, per * (t - 7), t + 2))

        @pl.when(middle)
        def _():
            lax.fori_loop(last_rest(t - 1), last_rest(t), do_rest, 0)

    total[...] = jnp.zeros_like(total)

    def amplitude_pass(source, first, groups, totals):
        def fetch(g, slot):
            return pltpu.make_async_copy(
                source.at[:, pl.ds(pl.multiple_of(first + g * 8, 8), 8), :], tbuf.at[slot], tsem.at[slot])

        fetch(0, 0).start()

        @pl.loop(0, groups)
        def _(g):
            slot = g % 2

            @pl.when(g + 1 < groups)
            def _():
                fetch(g + 1, 1 - slot).start()

            fetch(g, slot).wait()
            flat = tbuf.at[slot].reshape(count_c * 8, tbuf.shape[-1])
            part = jnp.zeros(total.shape, jnp.float32)
            for d in range(8):
                t_hi, t_lo = split(flat[pl.ds(d, count_c, stride=8), :])
                rows = pl.ds(pl.multiple_of((g * 8 + d) * count_b, count_b), count_b)
                wide = totals[rows, :]
                tall = jnp.concatenate(
                    [wide[:, a * count_c:(a + 1) * count_c] for a in range(count_a)], axis=0)
                x_hi, x_lo = split(tall)
                part += jnp.dot(
                    jnp.concatenate([x_hi, x_hi, x_lo], axis=1),
                    jnp.concatenate([t_hi, t_lo, t_hi], axis=0),
                    preferred_element_type=jnp.float32)
            total[...] += part

    amplitude_pass(amps, 0, main // 8, acc)

    @pl.when(middle)
    def _():
        amplitude_pass(amps, main, rest // 8, own_rest)
        te_copy().wait_recv()
        amplitude_pass(te, 0, rest // 8, far_rest)

    total[...] = total[...].T

    size = out.shape[0]

    def d_copy(step, src_rows, slot, who):
        return remote(total.at[pl.ds(pl.multiple_of(src_rows * size, size), size)], red_d.at[slot],
                      d_send.at[step], d_recv.at[step], (i, who))

    for step in range(1, nd):
        to = (j + step) % nd
        d_copy(step, to, step, to).start()
    red_d[0] = total[pl.ds(pl.multiple_of(j * size, size), size), :]
    for step in range(1, nd):
        d_copy(step, j, step, js).wait_recv()
    here = red_d[0]
    for step in range(1, nd):
        here = here + red_d[step]
    red_c[0] = here

    def c_copy(step):
        return remote(red_c.at[0], red_c.at[step], c_send.at[step], c_recv.at[step], ((i + step) % nz, j))

    for step in range(1, nz):
        c_copy(step).start()
    for step in range(1, nz):
        c_copy(step).wait_recv()
    for step in range(1, nz):
        here = here + red_c[step]
    out[...] = here

    for step in range(1, nz):
        c_copy(step).wait_send()
    for step in range(1, nd):
        d_copy(step, j, step, js).wait_send()
    for n in range(8):
        lg_copy(0, n).wait_send()

    @pl.when(middle)
    def _():
        for n in range(8):
            lg_copy(1, n).wait_send()

    @pl.when(is_end)
    def _():
        for h in (0, 1):
            le_copy(h).wait_send()
        for k in range(per):
            e_copy(k).wait_send()
        te_copy().wait_send()

    for way in (0, 1):
        @pl.when(n_send[way] > 0)
        def _(way=way):
            for n in range(AHEAD):
                z_wait_send(way, n_send[way] - AHEAD + n)


def shards(nz, nd, main, vectors_left, vectors_right, amplitudes):
    count_a, count_c, left_q = vectors_left.shape
    count_b, count_d, right_q = vectors_right.shape
    pairs = amplitudes.shape[2]
    rest = count_d - main
    per = right_q // CHUNK
    f32, bf16 = jnp.float32, jnp.bfloat16
    columns = count_a * count_c
    dma = pltpu.SemaphoreType.DMA
    hbm = pl.BlockSpec(memory_space=pl.ANY)
    results = pl.pallas_call(
        functools.partial(kernel, nz, nd, main),
        out_shape=[
            jax.ShapeDtypeStruct((pairs // nd, count_a * count_b), f32),
            jax.ShapeDtypeStruct((2, nd, count_a, count_c, left_q), f32),
            jax.ShapeDtypeStruct((nz, count_d, count_b, right_q), f32),
            jax.ShapeDtypeStruct((count_c, rest, pairs), f32),
        ],
        in_specs=[hbm] * 3,
        out_specs=[pl.BlockSpec(memory_space=pltpu.VMEM), hbm, hbm, hbm],
        scratch_shapes=[
            pltpu.VMEM((main * count_b, columns), f32),
            pltpu.VMEM((rest * count_b, columns), f32),
            pltpu.VMEM((rest * count_b, columns), f32),
            pltpu.VMEM((count_a, count_c, CHUNK), f32),
            pltpu.VMEM((main, count_b, CHUNK), f32),
            pltpu.VMEM((columns, 3 * CHUNK), bf16),
            pltpu.VMEM((main * count_b, 3 * CHUNK), bf16),
            pltpu.VMEM((2, count_c, 8, pairs), f32),
            pltpu.VMEM((count_a * count_b, pairs), f32),
            pltpu.VMEM((nd, pairs // nd, count_a * count_b), f32),
            pltpu.VMEM((nz, pairs // nd, count_a * count_b), f32),
            dma((2, (nz - 1) * per)), dma((2, (nz - 1) * per)),
            dma((2 * per,)), dma((2 * per,)),
            dma((per,)), dma((per,)),
            dma((2,)), dma((2,)),
            dma, dma,
            dma((2, 8)), dma((2, 8)),
            dma((nd,)), dma((nd,)),
            dma((nz,)), dma((nz,)),
            dma((2,)), dma((2,)),
        ],
        compiler_params=pltpu.CompilerParams(
            collective_id=0, has_side_effects=True, vmem_limit_bytes=52 * 2**20),
        name="ladder",
    )(vectors_left, jnp.transpose(vectors_right, (1, 0, 2)), amplitudes)
    whole = results[0].reshape(pairs // nd, count_a, count_b)
    width = count_b // nz
    return lax.dynamic_slice_in_dim(whole, lax.axis_index("vc") * width, width, axis=2)


def solution(mesh):
    nz, nd = mesh.shape["vc"], mesh.shape["vd"]
    fits = nz == 4 and nd == 8
    body = functools.partial(shards, nz, nd, 88) if fits else plain
    return jax.shard_map(
        body,
        mesh=mesh,
        in_specs=(P(None, "vc", "vd"), P(None, "vd", "vc"), P("vc", "vd", None)),
        out_specs=P("vd", None, "vc"),
        check_vma=False,
    )
```

```python
import functools

import jax
import jax.numpy as jnp
from jax import lax
from jax.experimental import pallas as pl
from jax.experimental.pallas import tpu as pltpu
from jax.sharding import PartitionSpec as P

MESH = pl.DeviceIdType.MESH
CHUNK = 256
AHEAD = 3
AHEAD_REST = 2


def contract(left_rows, right_rows):
    return lax.dot_general(
        left_rows,
        right_rows,
        (((1,), (1,)), ((), ())),
        precision=lax.Precision.HIGHEST,
        preferred_element_type=jnp.float32,
    )


def plain(vectors_left, vectors_right, amplitudes):
    count_a, count_c, left_q = vectors_left.shape
    count_b, count_d, right_q = vectors_right.shape
    left_whole = lax.all_gather(vectors_left, "vd", axis=2, tiled=True)
    left_flat = left_whole.reshape(count_a * count_c, left_whole.shape[2])
    piece = lax.all_gather(vectors_right, "vc", axis=2, tiled=True)
    width = piece.shape[2]
    tile = contract(left_flat, piece.reshape(count_b * count_d, width))
    tile = tile.reshape(count_a, count_c, count_b, count_d)
    partial_sum = jnp.einsum("acbd,cdi->iab", tile, amplitudes, precision=lax.Precision.HIGHEST)
    reduced = lax.psum_scatter(partial_sum, "vd", scatter_dimension=0, tiled=True)
    return lax.psum_scatter(reduced, "vc", scatter_dimension=2, tiled=True)


def split(x):
    hi = x.astype(jnp.bfloat16)
    lo = (x - hi.astype(jnp.float32)).astype(jnp.bfloat16)
    return hi, lo


def kernel(nz, nd, main, left, right, amps, out, lg, rg, te, acc, own_rest, far_rest,
           lbuf, rbuf, ls, rs, tbuf, total, red_d, red_c,
           z_send, z_recv, m_send, m_recv, e_send, e_recv, le_send, le_recv, te_send, te_recv,
           lg_send, lg_recv, d_send, d_recv, c_send, c_recv, local, tsem, keep):
    count_a, count_c, left_q = left.shape
    count_d, count_b, right_q = right.shape
    per = right_q // CHUNK
    rest = count_d - main
    halves = left_q // CHUNK
    rows_main, rows_rest = main * count_b, rest * count_b
    i = lax.axis_index("vc")
    j = lax.axis_index("vd")
    core, x, y = j % 2, (j // 2) % 2, j // 4
    jx, jy, js = j + 2 - 4 * x, j + 4 - 8 * y, j + 1 - 2 * core
    jd = jx + 4 - 8 * y
    is_end = (i == 0) | (i == nz - 1)
    middle = jnp.logical_not(is_end)
    low = i < nz // 2
    partner = jnp.where(low, 1 - i, 2 * nz - 3 - i)
    across = nz - 1 - i

    barrier = pltpu.get_barrier_semaphore()
    for step in range(1, nd):
        pl.semaphore_signal(barrier, inc=1, device_id=(i, (j + step) % nd), device_id_type=MESH)
    for step in range(1, nz):
        pl.semaphore_signal(barrier, inc=1, device_id=((i + step) % nz, j), device_id_type=MESH)
    pl.semaphore_wait(barrier, nd - 1 + nz - 1)

    def remote(src, dst, send, recv, who):
        return pltpu.make_async_remote_copy(
            src_ref=src, dst_ref=dst, send_sem=send, recv_sem=recv, device_id=who, device_id_type=MESH)

    n_send = (jnp.where(i < nz - 1, per * (i + 1), 0), jnp.where(i > 0, per * (nz - i), 0))
    n_recv = (per * i, per * (nz - 1 - i))

    def mine(k, start, size):
        cols = pl.ds(pl.multiple_of(k * CHUNK, CHUNK), CHUNK)
        return right.at[pl.ds(start, size), :, cols]

    def z_copy(way, n, src_own):
        block = jnp.where(way == 0, i - n // per, i + n // per) if src_own is None else i
        dst = rg.at[block, n % per, pl.ds(0, main)]
        src = mine(n % per, 0, main) if src_own else dst
        who = (i + 1, j) if way == 0 else (i - 1, j)
        return remote(src, dst, z_send.at[way, n], z_recv.at[way, n], who)

    def z_start(way, n):
        @pl.when((n < per) & (n < n_send[way]))
        def _():
            z_copy(way, n, True).start()

        @pl.when((n >= per) & (n < n_send[way]))
        def _():
            z_copy(way, n, None).start()

    def z_wait_recv(way, n):
        block = i - 1 - n // per if way == 0 else i + 1 + n // per
        dst = rg.at[block, n % per, pl.ds(0, main)]
        remote(dst, dst, z_send.at[way, n], z_recv.at[way, n], (partner, j)).wait_recv()

    def z_wait_send(way, n):
        src = mine(n % per, 0, main)
        remote(src, src, z_send.at[way, n], z_recv.at[way, n], (partner, j)).wait_send()

    def e_copy(k):
        return remote(mine(k, main, rest), rg.at[i, k, pl.ds(main, rest)],
                      e_send.at[k], e_recv.at[k], (partner, j))

    def m_start(r):
        @pl.when(r < per)
        def _():
            remote(mine(r % per, main, rest), rg.at[i, r % per, pl.ds(main, rest)],
                   m_send.at[r], m_recv.at[r], (across, j)).start()

        @pl.when((r >= per) & (r < 2 * per))
        def _():
            block = rg.at[partner, r % per, pl.ds(main, rest)]
            remote(block, block, m_send.at[r], m_recv.at[r], (across, j)).start()

    def m_copy(r):
        block = jnp.where(r < per, across, nz - 1 - partner)
        ref = rg.at[block, r % per, pl.ds(main, rest)]
        return remote(ref, ref, m_send.at[r], m_recv.at[r], (across, j))

    def le_copy(h):
        return remote(lg.at[0, j, h], lg.at[1, j, h],
                      le_send.at[h], le_recv.at[h], (partner, j))

    def te_copy():
        return remote(amps.at[:, pl.ds(main, rest), :], te, te_send, te_recv, (partner, j))

    def lg_copy(g, n):
        h0, h1 = pl.ds(0, halves // 2), pl.ds(halves // 2, halves // 2)
        src, to = (
            (lg.at[g, j], jx), (lg.at[g, j], jy), (lg.at[g, j], js),
            (lg.at[g, jx, h0], jy), (lg.at[g, jy, h1], jx),
            (lg.at[g, jx], js), (lg.at[g, jy], js), (lg.at[g, jd], js),
        )[n]
        return remote(src, src, lg_send.at[g, n], lg_recv.at[g, n], (i, to))

    def lg_first(g):
        for n in (0, 1, 2):
            lg_copy(g, n).start()

    def lg_second(g):
        for n in (0, 1):
            lg_copy(g, n).wait_recv()
        for n in (3, 4, 5, 6):
            lg_copy(g, n).start()

    def lg_third(g):
        for n in (3, 4):
            lg_copy(g, n).wait_recv()
        lg_copy(g, 7).start()

    def lg_last(g):
        for n in (2, 5, 6, 7):
            lg_copy(g, n).wait_recv()

    def load_left(g, block, k):
        chunk = block * per + k
        src = lg.at[g, chunk // halves, chunk % halves]
        return pltpu.make_async_copy(src, lbuf, local.at[0])

    def load_right(block, k, start, size):
        src = rg.at[block, k, pl.ds(start, size)]
        return pltpu.make_async_copy(src, rbuf.at[pl.ds(0, size)], local.at[1])

    def split_left():
        @pl.loop(0, count_a)
        def _(a):
            hi, lo = split(lbuf[a])
            cols = pl.ds(pl.multiple_of(a * count_c, count_c), count_c)
            ls[0:CHUNK, cols] = hi
            ls[CHUNK:2 * CHUNK, cols] = lo
            ls[2 * CHUNK:3 * CHUNK, cols] = hi

    def split_right(size):
        @pl.loop(0, size // 8)
        def _(g):
            hi, lo = split(rbuf[pl.ds(g * 8, 8)].reshape(8 * count_b, CHUNK))
            rows = pl.ds(pl.multiple_of(g * 8 * count_b, 8 * count_b), 8 * count_b)
            rs[rows, 0:CHUNK] = hi
            rs[rows, CHUNK:2 * CHUNK] = hi
            rs[rows, 2 * CHUNK:3 * CHUNK] = lo

    def multiply(target, rows):
        parts = 2 if rows > 1024 else 1
        size = rows // parts

        @pl.loop(0, count_a)
        def _(a):
            cols = pl.ds(pl.multiple_of(a * count_c, count_c), count_c)
            for part in range(parts):
                span = pl.ds(part * size, size)
                target[span, cols] += jnp.dot(
                    rs[span, :], ls[:, cols], preferred_element_type=jnp.float32)

    def main_task(block, k):
        a, b = load_left(0, block, k), load_right(block, k, 0, main)
        a.start()
        b.start()
        a.wait()
        split_left()
        b.wait()
        split_right(main)
        multiply(acc, rows_main)

    def rest_task(block, k):
        b = load_right(block, k, main, rest)
        b.start()
        a = load_left(0, block, k)
        a.start()
        b.wait()
        split_right(rest)
        a.wait()
        split_left()
        a = load_left(1, block, k)
        a.start()
        multiply(own_rest, rows_rest)
        a.wait()
        split_left()
        multiply(far_rest, rows_rest)

    for way in (0, 1):
        for n in range(AHEAD):
            z_start(way, n)
    keep_right = [pltpu.make_async_copy(mine(k, 0, count_d), rg.at[i, k], keep.at[k]) for k in range(per)]
    for copy in keep_right:
        copy.start()

    for h in range(halves):
        take = pltpu.make_async_copy(left.at[:, :, pl.ds(h * CHUNK, CHUNK)], lbuf, local.at[0])
        take.start()
        take.wait()

        @pl.loop(0, count_a)
        def _(a):
            lbuf[a] = lbuf[a].T

        give = pltpu.make_async_copy(lbuf, lg.at[0, j, h], local.at[0])
        give.start()
        give.wait()

        @pl.when(is_end)
        def _(h=h):
            le_copy(h).start()

    lg_first(0)

    @pl.loop(0, count_a)
    def _(a):
        cols = pl.ds(pl.multiple_of(a * count_c, count_c), count_c)
        acc[:, cols] = jnp.zeros((rows_main, count_c), jnp.float32)
        own_rest[:, cols] = jnp.zeros((rows_rest, count_c), jnp.float32)
        far_rest[:, cols] = jnp.zeros((rows_rest, count_c), jnp.float32)

    for copy in keep_right:
        copy.wait()

    steps = (nz - 1) * per

    def last_task(t):
        return jnp.where(t < 5, 0, jnp.minimum(jnp.minimum(per + 6 * (t - 5), per + 2 * (t + 1)), per + 2 * steps))

    @pl.loop(0, 15)
    def _(t):
        for way in (0, 1):
            @pl.when(t < n_recv[way])
            def _(way=way):
                z_wait_recv(way, t)

        for way in (0, 1):
            @pl.when(t + AHEAD < n_send[way])
            def _(way=way):
                z_wait_send(way, t)

            z_start(way, t + AHEAD)

        @pl.when(is_end)
        def _():
            @pl.when(t == 3)
            def _():
                for k in range(2):
                    e_copy(k).start()

            @pl.when(t == 4)
            def _():
                for k in range(2, per):
                    e_copy(k).start()

            @pl.when(t == 6)
            def _():
                te_copy().start()

        @pl.when(t == 2)
        def _():
            lg_second(0)

        @pl.when((t == 3) & middle)
        def _():
            for h in range(halves):
                le_copy(h).wait_recv()
            lg_first(1)

        @pl.when(t == 4)
        def _():
            lg_third(0)

        @pl.when(t == 5)
        def _():
            lg_last(0)

        @pl.when(middle)
        def _():
            @pl.when(t == 5)
            def _():
                lg_second(1)

            @pl.when(t == 6)
            def _():
                for r in range(AHEAD_REST):
                    m_start(r)

            @pl.when(t == 7)
            def _():
                lg_third(1)

            @pl.when(t == 8)
            def _():
                lg_last(1)

            @pl.when(t == 9)
            def _():
                for k in range(per):
                    e_copy(k).wait_recv()

            @pl.when(t >= 7)
            def _():
                m_copy(t - 7).wait_send()
                m_start(t - 7 + AHEAD_REST)
                m_copy(t - 7).wait_recv()

        def do_main(q, carry):
            u, way = (q - per) // 2, (q - per) % 2
            own = q < per
            block = jnp.where(own, i, jnp.where(way == 0, i - 1 - u // per, i + 1 + u // per))
            k = jnp.where(own, q, u % per)

            @pl.when(own | (u < jnp.where(way == 0, n_recv[0], n_recv[1])))
            def _():
                main_task(block, k)

            return carry

        lax.fori_loop(last_task(t - 1), last_task(t), do_main, 0)

        def do_rest(p, carry):
            source = p // per
            block = jnp.where(source == 0, i, jnp.where(source == 1, partner, jnp.where(
                source == 2, across, nz - 1 - partner)))
            rest_task(block, p % per)
            return carry

        def last_rest(t):
            return jnp.where(t < 8, 0, jnp.where(t < 11, per * (t - 7), t + 2))

        @pl.when(middle)
        def _():
            lax.fori_loop(last_rest(t - 1), last_rest(t), do_rest, 0)

    total[...] = jnp.zeros_like(total)

    def amplitude_pass(source, first, groups, totals):
        def fetch(g, slot):
            return pltpu.make_async_copy(
                source.at[:, pl.ds(pl.multiple_of(first + g * 8, 8), 8), :], tbuf.at[slot], tsem.at[slot])

        fetch(0, 0).start()

        @pl.loop(0, groups)
        def _(g):
            slot = g % 2

            @pl.when(g + 1 < groups)
            def _():
                fetch(g + 1, 1 - slot).start()

            fetch(g, slot).wait()
            flat = tbuf.at[slot].reshape(count_c * 8, tbuf.shape[-1])
            part = jnp.zeros(total.shape, jnp.float32)
            for d in range(8):
                t_hi, t_lo = split(flat[pl.ds(d, count_c, stride=8), :])
                rows = pl.ds(pl.multiple_of((g * 8 + d) * count_b, count_b), count_b)
                wide = totals[rows, :]
                tall = jnp.concatenate(
                    [wide[:, a * count_c:(a + 1) * count_c] for a in range(count_a)], axis=0)
                x_hi, x_lo = split(tall)
                part += jnp.dot(
                    jnp.concatenate([x_hi, x_hi, x_lo], axis=1),
                    jnp.concatenate([t_hi, t_lo, t_hi], axis=0),
                    preferred_element_type=jnp.float32)
            total[...] += part

    amplitude_pass(amps, 0, main // 8, acc)

    @pl.when(middle)
    def _():
        amplitude_pass(amps, main, rest // 8, own_rest)
        te_copy().wait_recv()
        amplitude_pass(te, 0, rest // 8, far_rest)

    total[...] = total[...].T

    size = out.shape[0]

    def d_copy(step, src_rows, slot, who):
        return remote(total.at[pl.ds(pl.multiple_of(src_rows * size, size), size)], red_d.at[slot],
                      d_send.at[step], d_recv.at[step], (i, who))

    for step in range(1, nd):
        to = (j + step) % nd
        d_copy(step, to, step, to).start()
    red_d[0] = total[pl.ds(pl.multiple_of(j * size, size), size), :]
    for step in range(1, nd):
        d_copy(step, j, step, js).wait_recv()
    here = red_d[0]
    for step in range(1, nd):
        here = here + red_d[step]
    red_c[0] = here

    def c_copy(step):
        return remote(red_c.at[0], red_c.at[step], c_send.at[step], c_recv.at[step], ((i + step) % nz, j))

    for step in range(1, nz):
        c_copy(step).start()
    for step in range(1, nz):
        c_copy(step).wait_recv()
    for step in range(1, nz):
        here = here + red_c[step]
    out[...] = here

    for step in range(1, nz):
        c_copy(step).wait_send()
    for step in range(1, nd):
        d_copy(step, j, step, js).wait_send()
    for n in range(8):
        lg_copy(0, n).wait_send()

    @pl.when(middle)
    def _():
        for n in range(8):
            lg_copy(1, n).wait_send()

    @pl.when(is_end)
    def _():
        for h in range(halves):
            le_copy(h).wait_send()
        for k in range(per):
            e_copy(k).wait_send()
        te_copy().wait_send()

    for way in (0, 1):
        @pl.when(n_send[way] > 0)
        def _(way=way):
            for n in range(AHEAD):
                z_wait_send(way, n_send[way] - AHEAD + n)


def shards(nz, nd, main, vectors_left, vectors_right, amplitudes):
    count_a, count_c, left_q = vectors_left.shape
    count_b, count_d, right_q = vectors_right.shape
    pairs = amplitudes.shape[2]
    rest = count_d - main
    per = right_q // CHUNK
    f32, bf16 = jnp.float32, jnp.bfloat16
    columns = count_a * count_c
    dma = pltpu.SemaphoreType.DMA
    hbm = pl.BlockSpec(memory_space=pl.ANY)
    results = pl.pallas_call(
        functools.partial(kernel, nz, nd, main),
        out_shape=[
            jax.ShapeDtypeStruct((pairs // nd, count_a * count_b), f32),
            jax.ShapeDtypeStruct((2, nd, left_q // CHUNK, count_a, CHUNK, count_c), f32),
            jax.ShapeDtypeStruct((nz, per, count_d, count_b, CHUNK), f32),
            jax.ShapeDtypeStruct((count_c, rest, pairs), f32),
        ],
        in_specs=[hbm] * 3,
        out_specs=[pl.BlockSpec(memory_space=pltpu.VMEM), hbm, hbm, hbm],
        scratch_shapes=[
            pltpu.VMEM((main * count_b, columns), f32),
            pltpu.VMEM((rest * count_b, columns), f32),
            pltpu.VMEM((rest * count_b, columns), f32),
            pltpu.VMEM((count_a, CHUNK, count_c), f32),
            pltpu.VMEM((main, count_b, CHUNK), f32),
            pltpu.VMEM((3 * CHUNK, columns), bf16),
            pltpu.VMEM((main * count_b, 3 * CHUNK), bf16),
            pltpu.VMEM((2, count_c, 8, pairs), f32),
            pltpu.VMEM((count_a * count_b, pairs), f32),
            pltpu.VMEM((nd, pairs // nd, count_a * count_b), f32),
            pltpu.VMEM((nz, pairs // nd, count_a * count_b), f32),
            dma((2, (nz - 1) * per)), dma((2, (nz - 1) * per)),
            dma((2 * per,)), dma((2 * per,)),
            dma((per,)), dma((per,)),
            dma((2,)), dma((2,)),
            dma, dma,
            dma((2, 8)), dma((2, 8)),
            dma((nd,)), dma((nd,)),
            dma((nz,)), dma((nz,)),
            dma((2,)), dma((2,)), dma((per,)),
        ],
        compiler_params=pltpu.CompilerParams(
            collective_id=0, has_side_effects=True, vmem_limit_bytes=52 * 2**20),
        name="ladder",
    )(vectors_left, jnp.transpose(vectors_right, (1, 0, 2)), amplitudes)
    whole = results[0].reshape(pairs // nd, count_a, count_b)
    width = count_b // nz
    return lax.dynamic_slice_in_dim(whole, lax.axis_index("vc") * width, width, axis=2)


def solution(mesh):
    nz, nd = mesh.shape["vc"], mesh.shape["vd"]
    fits = nz == 4 and nd == 8
    body = functools.partial(shards, nz, nd, 88) if fits else plain
    return jax.shard_map(
        body,
        mesh=mesh,
        in_specs=(P(None, "vc", "vd"), P(None, "vd", "vc"), P("vc", "vd", None)),
        out_specs=P("vd", None, "vc"),
        check_vma=False,
    )
```

```python
import functools

import jax
import jax.numpy as jnp
from jax import lax
from jax.experimental import pallas as pl
from jax.experimental.pallas import tpu as pltpu
from jax.sharding import PartitionSpec as P

MESH = pl.DeviceIdType.MESH
CHUNK = 256
AHEAD = 2


def contract(left_rows, right_rows):
    return lax.dot_general(
        left_rows,
        right_rows,
        (((1,), (1,)), ((), ())),
        precision=lax.Precision.HIGHEST,
        preferred_element_type=jnp.float32,
    )


def plain(vectors_left, vectors_right, amplitudes):
    count_a, count_c, left_q = vectors_left.shape
    count_b, count_d, right_q = vectors_right.shape
    left_whole = lax.all_gather(vectors_left, "vd", axis=2, tiled=True)
    left_flat = left_whole.reshape(count_a * count_c, left_whole.shape[2])
    piece = lax.all_gather(vectors_right, "vc", axis=2, tiled=True)
    width = piece.shape[2]
    tile = contract(left_flat, piece.reshape(count_b * count_d, width))
    tile = tile.reshape(count_a, count_c, count_b, count_d)
    partial_sum = jnp.einsum("acbd,cdi->iab", tile, amplitudes, precision=lax.Precision.HIGHEST)
    reduced = lax.psum_scatter(partial_sum, "vd", scatter_dimension=0, tiled=True)
    return lax.psum_scatter(reduced, "vc", scatter_dimension=2, tiled=True)


def split(x):
    hi = x.astype(jnp.bfloat16)
    lo = (x - hi.astype(jnp.float32)).astype(jnp.bfloat16)
    return hi, lo


def kernel(nz, nd, main, left, right, amps, out, lg, rg, te, acc, far,
           lbuf, rbuf, ls, rs, tbuf, total, red_d, red_c,
           in_send, in_recv, m_send, m_recv, e_send, e_recv, le_send, le_recv, te_send, te_recv,
           lg_send, lg_recv, d_send, d_recv, c_send, c_recv, local, tsem, keep):
    count_a, count_c, left_q = left.shape
    count_d, count_b, right_q = right.shape
    per = right_q // CHUNK
    rest = count_d - main
    halves = left_q // CHUNK
    rows_main, rows_rest = main * count_b, rest * count_b
    i = lax.axis_index("vc")
    j = lax.axis_index("vd")
    core, x, y = j % 2, (j // 2) % 2, j // 4
    jx, jy, js = j + 2 - 4 * x, j + 4 - 8 * y, j + 1 - 2 * core
    jd = jx + 4 - 8 * y
    is_end = (i == 0) | (i == nz - 1)
    middle = jnp.logical_not(is_end)
    partner = jnp.where(i < nz // 2, 1 - i, 2 * nz - 3 - i)
    across = nz - 1 - i

    barrier = pltpu.get_barrier_semaphore()
    for step in range(1, nd):
        pl.semaphore_signal(barrier, inc=1, device_id=(i, (j + step) % nd), device_id_type=MESH)
    for step in range(1, nz):
        pl.semaphore_signal(barrier, inc=1, device_id=((i + step) % nz, j), device_id_type=MESH)
    pl.semaphore_wait(barrier, nd - 1 + nz - 1)

    def remote(src, dst, send, recv, who):
        return pltpu.make_async_remote_copy(
            src_ref=src, dst_ref=dst, send_sem=send, recv_sem=recv, device_id=who, device_id_type=MESH)

    def mine(k, start, size):
        cols = pl.ds(pl.multiple_of(k * CHUNK, CHUNK), CHUNK)
        return right.at[pl.ds(start, size), :, cols]

    def in_copy(n, own):
        dst = rg.at[jnp.where(n < per, i, jnp.where(n < 2 * per, across, nz - 1 - partner)), n % per, pl.ds(0, main)]
        return remote(mine(n, 0, main) if own else dst, dst, in_send.at[n], in_recv.at[n], (partner, j))

    def e_copy(k):
        return remote(mine(k, 0, count_d), rg.at[i, k], e_send.at[k], e_recv.at[k], (partner, j))

    def m_start(n):
        @pl.when(n < per)
        def _():
            remote(mine(n, 0, count_d), rg.at[i, n], m_send.at[n], m_recv.at[n], (across, j)).start()

        @pl.when(n >= per)
        def _():
            block = rg.at[partner, n % per]
            remote(block, block, m_send.at[n], m_recv.at[n], (across, j)).start()

    def m_copy(n):
        ref = rg.at[jnp.where(n < per, across, nz - 1 - partner), n % per]
        return remote(ref, ref, m_send.at[n], m_recv.at[n], (across, j))

    def le_copy(h):
        return remote(lg.at[0, j, h], lg.at[1, j, h],
                      le_send.at[h], le_recv.at[h], (partner, j))

    def te_copy():
        return remote(amps.at[:, pl.ds(main, rest), :], te, te_send, te_recv, (partner, j))

    def lg_copy(g, n):
        h0, h1 = pl.ds(0, halves // 2), pl.ds(halves // 2, halves // 2)
        src, to = (
            (lg.at[g, j], jx), (lg.at[g, j], jy), (lg.at[g, j], js),
            (lg.at[g, jx, h0], jy), (lg.at[g, jy, h1], jx),
            (lg.at[g, jx], js), (lg.at[g, jy], js), (lg.at[g, jd], js),
        )[n]
        return remote(src, src, lg_send.at[g, n], lg_recv.at[g, n], (i, to))

    def lg_first(g):
        for n in (0, 1, 2):
            lg_copy(g, n).start()

    def lg_second(g):
        for n in (0, 1):
            lg_copy(g, n).wait_recv()
        for n in (3, 4, 5, 6):
            lg_copy(g, n).start()

    def lg_third(g):
        for n in (3, 4):
            lg_copy(g, n).wait_recv()
        lg_copy(g, 7).start()

    def lg_last(g):
        for n in (2, 5, 6, 7):
            lg_copy(g, n).wait_recv()

    def load_left(g, block, k):
        chunk = block * per + k
        src = lg.at[g, chunk // halves, chunk % halves]
        return pltpu.make_async_copy(src, lbuf, local.at[0])

    def load_right(block, k, start, size):
        src = rg.at[block, k, pl.ds(start, size)]
        return pltpu.make_async_copy(src, rbuf.at[pl.ds(start, size)], local.at[1 if start == 0 else 2])

    def split_left():
        @pl.loop(0, count_a)
        def _(a):
            hi, lo = split(lbuf[a])
            cols = pl.ds(pl.multiple_of(a * count_c, count_c), count_c)
            ls[0:CHUNK, cols] = hi
            ls[CHUNK:2 * CHUNK, cols] = lo
            ls[2 * CHUNK:3 * CHUNK, cols] = hi

    def split_right(start, size):
        @pl.loop(start // 8, (start + size) // 8)
        def _(g):
            hi, lo = split(rbuf[pl.ds(g * 8, 8)].reshape(8 * count_b, CHUNK))
            rows = pl.ds(pl.multiple_of(g * 8 * count_b, 8 * count_b), 8 * count_b)
            rs[rows, 0:CHUNK] = hi
            rs[rows, CHUNK:2 * CHUNK] = hi
            rs[rows, 2 * CHUNK:3 * CHUNK] = lo

    def multiply(target, spans):
        @pl.loop(0, count_a)
        def _(a):
            cols = pl.ds(pl.multiple_of(a * count_c, count_c), count_c)
            for start, first, size in spans:
                target[pl.ds(start, size), cols] += jnp.dot(
                    rs[pl.ds(first, size), :], ls[:, cols], preferred_element_type=jnp.float32)

    half = rows_main // 2
    main_spans = ((0, 0, half), (half, half, half))
    rest_spans = main_spans + ((rows_main, rows_main, rows_rest),)
    far_spans = ((0, rows_main, rows_rest),)

    def run(first, last, where, g, parts, target, spans):
        def loads(q):
            block, k = where(q)
            return [load_left(g, block, k)] + [load_right(block, k, *part) for part in parts]

        @pl.when(first < last)
        def _():
            for copy in loads(first):
                copy.start()

        def task(q, carry):
            for copy in loads(q):
                copy.wait()
            split_left()
            for part in parts:
                split_right(*part)

            @pl.when(q + 1 < last)
            def _():
                for copy in loads(q + 1):
                    copy.start()

            multiply(target, spans)
            return carry

        lax.fori_loop(first, last, task, 0)

    def from_middle(n):
        return jnp.where(n < per, across, nz - 1 - partner), n % per

    def from_partner(n):
        return jnp.where(i == 0, 1 + n // per, nz - 2 - n // per), n % per

    def end_task(q):
        block, k = from_partner(q - per)
        return jnp.where(q < per, i, block), jnp.where(q < per, q, k)

    def middle_task(q):
        r = q - per - 3
        from_end = (r >= 0) & (r < 7) & (r % 2 == 0)
        n = jnp.where(r < 0, q - per, jnp.where(r < 7, 3 + r // 2, q - 2 * per))
        block, k = from_middle(n)
        block, k = jnp.where(from_end, partner, block), jnp.where(from_end, r // 2, k)
        return jnp.where(q < per, i, block), jnp.where(q < per, q, k)

    def far_task(q):
        block, k = from_middle(q - 2 * per)
        return jnp.where(q < per, i, jnp.where(q < 2 * per, partner, block)), jnp.where(q < 2 * per, q % per, k)

    @pl.when(is_end)
    def _():
        e_copy(0).start()

    @pl.when(middle)
    def _():
        for n in range(AHEAD):
            m_start(n)
        for n in range(per):
            in_copy(n, True).start()

    keep_right = [pltpu.make_async_copy(mine(k, 0, count_d), rg.at[i, k], keep.at[k]) for k in range(per)]
    for copy in keep_right:
        copy.start()

    for h in range(halves):
        take = pltpu.make_async_copy(left.at[:, :, pl.ds(h * CHUNK, CHUNK)], lbuf, local.at[0])
        take.start()
        take.wait()

        @pl.loop(0, count_a)
        def _(a):
            lbuf[a] = lbuf[a].T

        give = pltpu.make_async_copy(lbuf, lg.at[0, j, h], local.at[0])
        give.start()
        give.wait()

        @pl.when(is_end)
        def _(h=h):
            le_copy(h).start()

    lg_first(0)

    @pl.loop(0, count_a)
    def _(a):
        cols = pl.ds(pl.multiple_of(a * count_c, count_c), count_c)
        acc[:, cols] = jnp.zeros((rows_main + rows_rest, count_c), jnp.float32)
        far[:, cols] = jnp.zeros((rows_rest, count_c), jnp.float32)

    for copy in keep_right:
        copy.wait()

    @pl.when(is_end)
    def _():
        @pl.loop(0, (nz - 1) * per)
        def _(t):
            block, k = from_partner(t)
            ref = rg.at[block, k, pl.ds(0, main)]
            remote(ref, ref, in_send.at[t], in_recv.at[t], (partner, j)).wait_recv()

            @pl.when(t == 2)
            def _():
                e_copy(1).start()
                lg_second(0)

            @pl.when(t == 3)
            def _():
                lg_third(0)

            @pl.when(t == 4)
            def _():
                e_copy(2).start()
                lg_last(0)

            @pl.when(t == 5)
            def _():
                e_copy(3).start()

            @pl.when(t == 7)
            def _():
                te_copy().start()

            def last(t):
                return jnp.where(t < 4, 0, jnp.minimum(t + 5, 4 * t - 10))

            run(last(t - 1), last(t), end_task, 0, ((0, main),), acc, main_spans)

    @pl.when(middle)
    def _():
        @pl.loop(0, 2 * per)
        def _(t):
            m_copy(t).wait_recv()
            in_copy(t + per, False).start()

            @pl.when(t + AHEAD < 2 * per)
            def _():
                m_copy(t).wait_send()

                @pl.when(t + AHEAD >= per)
                def _():
                    e_copy(t + AHEAD - per).wait_recv()

                m_start(t + AHEAD)

            @pl.when(t == 1)
            def _():
                lg_second(0)

            @pl.when(t == 2)
            def _():
                lg_third(0)
                for h in range(halves):
                    le_copy(h).wait_recv()
                lg_first(1)
                lg_last(0)

            @pl.when(t == 4)
            def _():
                lg_second(1)

            @pl.when(t == 5)
            def _():
                lg_third(1)
                lg_last(1)

            def last(t):
                late = jnp.where(t < 6, 4 + 2 * t, 9 + t)
                return jnp.where(t < 2, 0, jnp.where(t == 2, 7, late))

            def last_far(t):
                return jnp.where(t < 5, 0, jnp.where(t < 7, 5 * t - 19, 16))

            run(last(t - 1), last(t), middle_task, 0, ((0, main), (main, rest)), acc, rest_spans)
            run(last_far(t - 1), last_far(t), far_task, 1, ((main, rest),), far, far_spans)

    total[...] = jnp.zeros_like(total)

    def amplitude_pass(source, first, groups, totals):
        def fetch(g, slot):
            return pltpu.make_async_copy(
                source.at[:, pl.ds(pl.multiple_of(first + g * 8, 8), 8), :], tbuf.at[slot], tsem.at[slot])

        fetch(0, 0).start()

        @pl.loop(0, groups)
        def _(g):
            slot = g % 2

            @pl.when(g + 1 < groups)
            def _():
                fetch(g + 1, 1 - slot).start()

            fetch(g, slot).wait()
            flat = tbuf.at[slot].reshape(count_c * 8, tbuf.shape[-1])
            part = jnp.zeros(total.shape, jnp.float32)
            for d in range(8):
                t_hi, t_lo = split(flat[pl.ds(d, count_c, stride=8), :])
                rows = pl.ds(pl.multiple_of((g * 8 + d) * count_b, count_b), count_b)
                wide = totals[rows, :]
                tall = jnp.concatenate(
                    [wide[:, a * count_c:(a + 1) * count_c] for a in range(count_a)], axis=0)
                x_hi, x_lo = split(tall)
                part += jnp.dot(
                    jnp.concatenate([x_hi, x_hi, x_lo], axis=1),
                    jnp.concatenate([t_hi, t_lo, t_hi], axis=0),
                    preferred_element_type=jnp.float32)
            total[...] += part

    amplitude_pass(amps, 0, jnp.where(middle, count_d // 8, main // 8), acc)

    @pl.when(middle)
    def _():
        te_copy().wait_recv()
        amplitude_pass(te, 0, rest // 8, far)

    total[...] = total[...].T

    size = out.shape[0]

    def d_copy(step, src_rows, slot, who):
        return remote(total.at[pl.ds(pl.multiple_of(src_rows * size, size), size)], red_d.at[slot],
                      d_send.at[step], d_recv.at[step], (i, who))

    for step in range(1, nd):
        to = (j + step) % nd
        d_copy(step, to, step, to).start()
    red_d[0] = total[pl.ds(pl.multiple_of(j * size, size), size), :]
    for step in range(1, nd):
        d_copy(step, j, step, js).wait_recv()
    here = red_d[0]
    for step in range(1, nd):
        here = here + red_d[step]
    red_c[0] = here

    def c_copy(step):
        return remote(red_c.at[0], red_c.at[step], c_send.at[step], c_recv.at[step], ((i + step) % nz, j))

    for step in range(1, nz):
        c_copy(step).start()
    for step in range(1, nz):
        c_copy(step).wait_recv()
    for step in range(1, nz):
        here = here + red_c[step]
    out[...] = here

    for step in range(1, nz):
        c_copy(step).wait_send()
    for step in range(1, nd):
        d_copy(step, j, step, js).wait_send()
    for n in range(8):
        lg_copy(0, n).wait_send()

    @pl.when(middle)
    def _():
        for n in range(8):
            lg_copy(1, n).wait_send()
        for n in range(AHEAD):
            m_copy(2 * per - AHEAD + n).wait_send()
        for n in range((nz - 1) * per):
            in_copy(n, False).wait_send()

    @pl.when(is_end)
    def _():
        for h in range(halves):
            le_copy(h).wait_send()
        for k in range(per):
            e_copy(k).wait_send()
        te_copy().wait_send()


def shards(nz, nd, main, vectors_left, vectors_right, amplitudes):
    count_a, count_c, left_q = vectors_left.shape
    count_b, count_d, right_q = vectors_right.shape
    pairs = amplitudes.shape[2]
    rest = count_d - main
    per = right_q // CHUNK
    f32, bf16 = jnp.float32, jnp.bfloat16
    columns = count_a * count_c
    dma = pltpu.SemaphoreType.DMA
    hbm = pl.BlockSpec(memory_space=pl.ANY)
    results = pl.pallas_call(
        functools.partial(kernel, nz, nd, main),
        out_shape=[
            jax.ShapeDtypeStruct((pairs // nd, count_a * count_b), f32),
            jax.ShapeDtypeStruct((2, nd, left_q // CHUNK, count_a, CHUNK, count_c), f32),
            jax.ShapeDtypeStruct((nz, per, count_d, count_b, CHUNK), f32),
            jax.ShapeDtypeStruct((count_c, rest, pairs), f32),
        ],
        in_specs=[hbm] * 3,
        out_specs=[pl.BlockSpec(memory_space=pltpu.VMEM), hbm, hbm, hbm],
        scratch_shapes=[
            pltpu.VMEM((count_d * count_b, columns), f32),
            pltpu.VMEM((rest * count_b, columns), f32),
            pltpu.VMEM((count_a, CHUNK, count_c), f32),
            pltpu.VMEM((count_d, count_b, CHUNK), f32),
            pltpu.VMEM((3 * CHUNK, columns), bf16),
            pltpu.VMEM((count_d * count_b, 3 * CHUNK), bf16),
            pltpu.VMEM((2, count_c, 8, pairs), f32),
            pltpu.VMEM((count_a * count_b, pairs), f32),
            pltpu.VMEM((nd, pairs // nd, count_a * count_b), f32),
            pltpu.VMEM((nz, pairs // nd, count_a * count_b), f32),
            dma(((nz - 1) * per,)), dma(((nz - 1) * per,)),
            dma((2 * per,)), dma((2 * per,)),
            dma((per,)), dma((per,)),
            dma((2,)), dma((2,)),
            dma, dma,
            dma((2, 8)), dma((2, 8)),
            dma((nd,)), dma((nd,)),
            dma((nz,)), dma((nz,)),
            dma((3,)), dma((2,)), dma((per,)),
        ],
        compiler_params=pltpu.CompilerParams(
            collective_id=0, has_side_effects=True, vmem_limit_bytes=52 * 2**20),
        name="ladder",
    )(vectors_left, jnp.transpose(vectors_right, (1, 0, 2)), amplitudes)
    whole = results[0].reshape(pairs // nd, count_a, count_b)
    width = count_b // nz
    return lax.dynamic_slice_in_dim(whole, lax.axis_index("vc") * width, width, axis=2)


def solution(mesh):
    nz, nd = mesh.shape["vc"], mesh.shape["vd"]
    fits = nz == 4 and nd == 8
    body = functools.partial(shards, nz, nd, 88) if fits else plain
    return jax.shard_map(
        body,
        mesh=mesh,
        in_specs=(P(None, "vc", "vd"), P(None, "vd", "vc"), P("vc", "vd", None)),
        out_specs=P("vd", None, "vc"),
        check_vma=False,
    )
```

```python
import functools

import jax
import jax.numpy as jnp
from jax import lax
from jax.experimental import pallas as pl
from jax.experimental.pallas import tpu as pltpu
from jax.sharding import PartitionSpec as P

MESH = pl.DeviceIdType.MESH
CHUNK = 256
AHEAD = 2


def contract(left_rows, right_rows):
    return lax.dot_general(
        left_rows,
        right_rows,
        (((1,), (1,)), ((), ())),
        precision=lax.Precision.HIGHEST,
        preferred_element_type=jnp.float32,
    )


def plain(vectors_left, vectors_right, amplitudes):
    count_a, count_c, left_q = vectors_left.shape
    count_b, count_d, right_q = vectors_right.shape
    left_whole = lax.all_gather(vectors_left, "vd", axis=2, tiled=True)
    left_flat = left_whole.reshape(count_a * count_c, left_whole.shape[2])
    piece = lax.all_gather(vectors_right, "vc", axis=2, tiled=True)
    width = piece.shape[2]
    tile = contract(left_flat, piece.reshape(count_b * count_d, width))
    tile = tile.reshape(count_a, count_c, count_b, count_d)
    partial_sum = jnp.einsum("acbd,cdi->iab", tile, amplitudes, precision=lax.Precision.HIGHEST)
    reduced = lax.psum_scatter(partial_sum, "vd", scatter_dimension=0, tiled=True)
    return lax.psum_scatter(reduced, "vc", scatter_dimension=2, tiled=True)


def split(x):
    hi = x.astype(jnp.bfloat16)
    lo = (x - hi.astype(jnp.float32)).astype(jnp.bfloat16)
    return hi, lo


def kernel(nz, nd, main, left, right, amps, out, lg, rg, te, acc, far,
           lbuf, rbuf, ls, rs, tbuf, total, red_d, red_c,
           in_send, in_recv, m_send, m_recv, e_send, e_recv, le_send, le_recv, te_send, te_recv,
           lg_send, lg_recv, d_send, d_recv, c_send, c_recv, local, tsem, keep):
    count_a, count_c, left_q = left.shape
    count_d, count_b, right_q = right.shape
    per = right_q // CHUNK
    rest = count_d - main
    halves = left_q // CHUNK
    rows_main, rows_rest = main * count_b, rest * count_b
    i = lax.axis_index("vc")
    j = lax.axis_index("vd")
    core, x, y = j % 2, (j // 2) % 2, j // 4
    jx, jy, js = j + 2 - 4 * x, j + 4 - 8 * y, j + 1 - 2 * core
    jd = jx + 4 - 8 * y
    is_end = (i == 0) | (i == nz - 1)
    middle = jnp.logical_not(is_end)
    partner = jnp.where(i < nz // 2, 1 - i, 2 * nz - 3 - i)
    across = nz - 1 - i

    barrier = pltpu.get_barrier_semaphore()
    for step in range(1, nd):
        pl.semaphore_signal(barrier, inc=1, device_id=(i, (j + step) % nd), device_id_type=MESH)
    for step in range(1, nz):
        pl.semaphore_signal(barrier, inc=1, device_id=((i + step) % nz, j), device_id_type=MESH)
    pl.semaphore_wait(barrier, nd - 1 + nz - 1)

    def remote(src, dst, send, recv, who):
        return pltpu.make_async_remote_copy(
            src_ref=src, dst_ref=dst, send_sem=send, recv_sem=recv, device_id=who, device_id_type=MESH)

    def mine(k, start, size):
        cols = pl.ds(pl.multiple_of(k * CHUNK, CHUNK), CHUNK)
        return right.at[pl.ds(start, size), :, cols]

    def in_copy(n, own):
        dst = rg.at[jnp.where(n < per, i, jnp.where(n < 2 * per, across, nz - 1 - partner)), n % per, pl.ds(0, main)]
        return remote(mine(n, 0, main) if own else dst, dst, in_send.at[n], in_recv.at[n], (partner, j))

    def e_copy(k):
        return remote(mine(k, 0, count_d), rg.at[i, k], e_send.at[k], e_recv.at[k], (partner, j))

    def m_start(n):
        @pl.when(n < per)
        def _():
            remote(mine(n, 0, count_d), rg.at[i, n], m_send.at[n], m_recv.at[n], (across, j)).start()

        @pl.when(n >= per)
        def _():
            block = rg.at[partner, n % per]
            remote(block, block, m_send.at[n], m_recv.at[n], (across, j)).start()

    def m_copy(n):
        ref = rg.at[jnp.where(n < per, across, nz - 1 - partner), n % per]
        return remote(ref, ref, m_send.at[n], m_recv.at[n], (across, j))

    def le_copy(h):
        return remote(lg.at[0, j, h], lg.at[1, j, h],
                      le_send.at[h], le_recv.at[h], (partner, j))

    def te_copy():
        return remote(amps.at[:, pl.ds(main, rest), :], te, te_send, te_recv, (partner, j))

    def lg_copy(g, n):
        h0, h1 = pl.ds(0, halves // 2), pl.ds(halves // 2, halves // 2)
        src, to = (
            (lg.at[g, j], jx), (lg.at[g, j], jy), (lg.at[g, j], js),
            (lg.at[g, jx, h0], jy), (lg.at[g, jy, h1], jx),
            (lg.at[g, jx], js), (lg.at[g, jy], js), (lg.at[g, jd], js),
        )[n]
        return remote(src, src, lg_send.at[g, n], lg_recv.at[g, n], (i, to))

    def lg_first(g):
        for n in (0, 1, 2):
            lg_copy(g, n).start()

    def lg_second(g):
        for n in (0, 1):
            lg_copy(g, n).wait_recv()
        for n in (3, 4, 5, 6):
            lg_copy(g, n).start()

    def lg_third(g):
        for n in (3, 4):
            lg_copy(g, n).wait_recv()
        lg_copy(g, 7).start()

    def lg_last(g):
        for n in (2, 5, 6, 7):
            lg_copy(g, n).wait_recv()

    def load_left(g, block, k):
        chunk = block * per + k
        src = lg.at[g, chunk // halves, chunk % halves]
        return pltpu.make_async_copy(src, lbuf, local.at[0])

    def load_right(block, k, start, size):
        src = rg.at[block, k, pl.ds(start, size)]
        return pltpu.make_async_copy(src, rbuf.at[pl.ds(start, size)], local.at[1 if start == 0 else 2])

    def split_left():
        @pl.loop(0, count_a)
        def _(a):
            hi, lo = split(lbuf[a])
            cols = pl.ds(pl.multiple_of(a * count_c, count_c), count_c)
            ls[0:CHUNK, cols] = hi
            ls[CHUNK:2 * CHUNK, cols] = lo
            ls[2 * CHUNK:3 * CHUNK, cols] = hi

    def split_right(start, size):
        @pl.loop(start // 8, (start + size) // 8)
        def _(g):
            hi, lo = split(rbuf[pl.ds(g * 8, 8)].reshape(8 * count_b, CHUNK))
            rows = pl.ds(pl.multiple_of(g * 8 * count_b, 8 * count_b), 8 * count_b)
            rs[rows, 0:CHUNK] = hi
            rs[rows, CHUNK:2 * CHUNK] = hi
            rs[rows, 2 * CHUNK:3 * CHUNK] = lo

    def multiply(target, span):
        first, size, wide = span
        width = wide * count_c

        @pl.loop(0, count_a // wide)
        def _(a):
            cols = pl.ds(pl.multiple_of(a * width, width), width)
            target[0:size, cols] += jnp.dot(
                rs[pl.ds(first, size), :], ls[:, cols], preferred_element_type=jnp.float32)

    main_span = (0, rows_main, 2)
    whole_span = (0, rows_main + rows_rest, 2)
    far_span = (rows_main, rows_rest, 4)

    def run(first, last, where, g, parts, target, span):
        def loads(q):
            block, k = where(q)
            return [load_left(g, block, k)] + [load_right(block, k, *part) for part in parts]

        @pl.when(first < last)
        def _():
            for copy in loads(first):
                copy.start()

        def task(q, carry):
            for copy in loads(q):
                copy.wait()
            split_left()
            for part in parts:
                split_right(*part)

            @pl.when(q + 1 < last)
            def _():
                for copy in loads(q + 1):
                    copy.start()

            multiply(target, span)
            return carry

        lax.fori_loop(first, last, task, 0)

    def from_middle(n):
        return jnp.where(n < per, across, nz - 1 - partner), n % per

    def from_partner(n):
        return jnp.where(i == 0, 1 + n // per, nz - 2 - n // per), n % per

    def end_task(q):
        block, k = from_partner(q - per)
        return jnp.where(q < per, i, block), jnp.where(q < per, q, k)

    def middle_task(q):
        r = q - per - 3
        from_end = (r >= 0) & (r < 7) & (r % 2 == 0)
        n = jnp.where(r < 0, q - per, jnp.where(r < 7, 3 + r // 2, q - 2 * per))
        block, k = from_middle(n)
        block, k = jnp.where(from_end, partner, block), jnp.where(from_end, r // 2, k)
        return jnp.where(q < per, i, block), jnp.where(q < per, q, k)

    def far_task(q):
        block, k = from_middle(q - 2 * per)
        return jnp.where(q < per, i, jnp.where(q < 2 * per, partner, block)), jnp.where(q < 2 * per, q % per, k)

    @pl.when(is_end)
    def _():
        e_copy(0).start()

    @pl.when(middle)
    def _():
        for n in range(AHEAD):
            m_start(n)
        for n in range(per):
            in_copy(n, True).start()

    keep_right = [pltpu.make_async_copy(mine(k, 0, count_d), rg.at[i, k], keep.at[k]) for k in range(per)]
    for copy in keep_right:
        copy.start()

    for h in range(halves):
        take = pltpu.make_async_copy(left.at[:, :, pl.ds(h * CHUNK, CHUNK)], lbuf, local.at[0])
        take.start()
        take.wait()

        @pl.loop(0, count_a)
        def _(a):
            lbuf[a] = lbuf[a].T

        give = pltpu.make_async_copy(lbuf, lg.at[0, j, h], local.at[0])
        give.start()
        give.wait()

        @pl.when(is_end)
        def _(h=h):
            le_copy(h).start()

    lg_first(0)

    @pl.loop(0, count_a)
    def _(a):
        cols = pl.ds(pl.multiple_of(a * count_c, count_c), count_c)
        acc[:, cols] = jnp.zeros((rows_main + rows_rest, count_c), jnp.float32)
        far[:, cols] = jnp.zeros((rows_rest, count_c), jnp.float32)

    for copy in keep_right:
        copy.wait()

    @pl.when(is_end)
    def _():
        @pl.loop(0, (nz - 1) * per)
        def _(t):
            block, k = from_partner(t)
            ref = rg.at[block, k, pl.ds(0, main)]
            remote(ref, ref, in_send.at[t], in_recv.at[t], (partner, j)).wait_recv()

            @pl.when(t == 2)
            def _():
                e_copy(1).start()
                lg_second(0)

            @pl.when(t == 3)
            def _():
                lg_third(0)

            @pl.when(t == 4)
            def _():
                e_copy(2).start()
                lg_last(0)

            @pl.when(t == 5)
            def _():
                e_copy(3).start()

            @pl.when(t == 7)
            def _():
                te_copy().start()

            def last(t):
                return jnp.where(t < 4, 0, jnp.minimum(t + 5, 4 * t - 10))

            run(last(t - 1), last(t), end_task, 0, ((0, main),), acc, main_span)

    @pl.when(middle)
    def _():
        @pl.loop(0, 2 * per)
        def _(t):
            m_copy(t).wait_recv()
            in_copy(t + per, False).start()

            @pl.when(t + AHEAD < 2 * per)
            def _():
                m_copy(t).wait_send()

                @pl.when(t + AHEAD >= per)
                def _():
                    e_copy(t + AHEAD - per).wait_recv()

                m_start(t + AHEAD)

            @pl.when(t == 1)
            def _():
                lg_second(0)

            @pl.when(t == 2)
            def _():
                lg_third(0)
                for h in range(halves):
                    le_copy(h).wait_recv()
                lg_first(1)
                lg_last(0)

            @pl.when(t == 4)
            def _():
                lg_second(1)

            @pl.when(t == 5)
            def _():
                lg_third(1)
                lg_last(1)

            def last(t):
                late = jnp.where(t < 6, 4 + 2 * t, 9 + t)
                return jnp.where(t < 2, 0, jnp.where(t == 2, 7, late))

            def last_far(t):
                return jnp.where(t < 5, 0, jnp.where(t < 7, 5 * t - 19, 16))

            run(last(t - 1), last(t), middle_task, 0, ((0, main), (main, rest)), acc, whole_span)
            run(last_far(t - 1), last_far(t), far_task, 1, ((main, rest),), far, far_span)

    total[...] = jnp.zeros_like(total)

    def amplitude_pass(source, first, groups, totals):
        def fetch(g, slot):
            return pltpu.make_async_copy(
                source.at[:, pl.ds(pl.multiple_of(first + g * 8, 8), 8), :], tbuf.at[slot], tsem.at[slot])

        fetch(0, 0).start()

        @pl.loop(0, groups)
        def _(g):
            slot = g % 2

            @pl.when(g + 1 < groups)
            def _():
                fetch(g + 1, 1 - slot).start()

            fetch(g, slot).wait()
            flat = tbuf.at[slot].reshape(count_c * 8, tbuf.shape[-1])
            part = jnp.zeros(total.shape, jnp.float32)
            for d in range(8):
                t_hi, t_lo = split(flat[pl.ds(d, count_c, stride=8), :])
                rows = pl.ds(pl.multiple_of((g * 8 + d) * count_b, count_b), count_b)
                wide = totals[rows, :]
                tall = jnp.concatenate(
                    [wide[:, a * count_c:(a + 1) * count_c] for a in range(count_a)], axis=0)
                x_hi, x_lo = split(tall)
                part += jnp.dot(
                    jnp.concatenate([x_hi, x_hi, x_lo], axis=1),
                    jnp.concatenate([t_hi, t_lo, t_hi], axis=0),
                    preferred_element_type=jnp.float32)
            total[...] += part

    amplitude_pass(amps, 0, jnp.where(middle, count_d // 8, main // 8), acc)

    @pl.when(middle)
    def _():
        te_copy().wait_recv()
        amplitude_pass(te, 0, rest // 8, far)

    total[...] = total[...].T

    size = out.shape[0]

    def d_copy(step, src_rows, slot, who):
        return remote(total.at[pl.ds(pl.multiple_of(src_rows * size, size), size)], red_d.at[slot],
                      d_send.at[step], d_recv.at[step], (i, who))

    for step in range(1, nd):
        to = (j + step) % nd
        d_copy(step, to, step, to).start()
    red_d[0] = total[pl.ds(pl.multiple_of(j * size, size), size), :]
    for step in range(1, nd):
        d_copy(step, j, step, js).wait_recv()
    here = red_d[0]
    for step in range(1, nd):
        here = here + red_d[step]
    red_c[0] = here

    def c_copy(step):
        return remote(red_c.at[0], red_c.at[step], c_send.at[step], c_recv.at[step], ((i + step) % nz, j))

    for step in range(1, nz):
        c_copy(step).start()
    for step in range(1, nz):
        c_copy(step).wait_recv()
    for step in range(1, nz):
        here = here + red_c[step]
    out[...] = here

    for step in range(1, nz):
        c_copy(step).wait_send()
    for step in range(1, nd):
        d_copy(step, j, step, js).wait_send()
    for n in range(8):
        lg_copy(0, n).wait_send()

    @pl.when(middle)
    def _():
        for n in range(8):
            lg_copy(1, n).wait_send()
        for n in range(AHEAD):
            m_copy(2 * per - AHEAD + n).wait_send()
        for n in range((nz - 1) * per):
            in_copy(n, False).wait_send()

    @pl.when(is_end)
    def _():
        for h in range(halves):
            le_copy(h).wait_send()
        for k in range(per):
            e_copy(k).wait_send()
        te_copy().wait_send()


def shards(nz, nd, main, vectors_left, vectors_right, amplitudes):
    count_a, count_c, left_q = vectors_left.shape
    count_b, count_d, right_q = vectors_right.shape
    pairs = amplitudes.shape[2]
    rest = count_d - main
    per = right_q // CHUNK
    f32, bf16 = jnp.float32, jnp.bfloat16
    columns = count_a * count_c
    dma = pltpu.SemaphoreType.DMA
    hbm = pl.BlockSpec(memory_space=pl.ANY)
    results = pl.pallas_call(
        functools.partial(kernel, nz, nd, main),
        out_shape=[
            jax.ShapeDtypeStruct((pairs // nd, count_a * count_b), f32),
            jax.ShapeDtypeStruct((2, nd, left_q // CHUNK, count_a, CHUNK, count_c), f32),
            jax.ShapeDtypeStruct((nz, per, count_d, count_b, CHUNK), f32),
            jax.ShapeDtypeStruct((count_c, rest, pairs), f32),
        ],
        in_specs=[hbm] * 3,
        out_specs=[pl.BlockSpec(memory_space=pltpu.VMEM), hbm, hbm, hbm],
        scratch_shapes=[
            pltpu.VMEM((count_d * count_b, columns), f32),
            pltpu.VMEM((rest * count_b, columns), f32),
            pltpu.VMEM((count_a, CHUNK, count_c), f32),
            pltpu.VMEM((count_d, count_b, CHUNK), f32),
            pltpu.VMEM((3 * CHUNK, columns), bf16),
            pltpu.VMEM((count_d * count_b, 3 * CHUNK), bf16),
            pltpu.VMEM((2, count_c, 8, pairs), f32),
            pltpu.VMEM((count_a * count_b, pairs), f32),
            pltpu.VMEM((nd, pairs // nd, count_a * count_b), f32),
            pltpu.VMEM((nz, pairs // nd, count_a * count_b), f32),
            dma(((nz - 1) * per,)), dma(((nz - 1) * per,)),
            dma((2 * per,)), dma((2 * per,)),
            dma((per,)), dma((per,)),
            dma((2,)), dma((2,)),
            dma, dma,
            dma((2, 8)), dma((2, 8)),
            dma((nd,)), dma((nd,)),
            dma((nz,)), dma((nz,)),
            dma((3,)), dma((2,)), dma((per,)),
        ],
        compiler_params=pltpu.CompilerParams(
            collective_id=0, has_side_effects=True, vmem_limit_bytes=52 * 2**20),
        name="ladder",
    )(vectors_left, jnp.transpose(vectors_right, (1, 0, 2)), amplitudes)
    whole = results[0].reshape(pairs // nd, count_a, count_b)
    width = count_b // nz
    return lax.dynamic_slice_in_dim(whole, lax.axis_index("vc") * width, width, axis=2)


def solution(mesh):
    nz, nd = mesh.shape["vc"], mesh.shape["vd"]
    fits = nz == 4 and nd == 8
    body = functools.partial(shards, nz, nd, 96) if fits else plain
    return jax.shard_map(
        body,
        mesh=mesh,
        in_specs=(P(None, "vc", "vd"), P(None, "vd", "vc"), P("vc", "vd", None)),
        out_specs=P("vd", None, "vc"),
        check_vma=False,
    )
```

```python
import functools

import jax
import jax.numpy as jnp
from jax import lax
from jax.experimental import pallas as pl
from jax.experimental.pallas import tpu as pltpu
from jax.sharding import PartitionSpec as P

MESH = pl.DeviceIdType.MESH
CHUNK = 256
AHEAD = 2


def contract(left_rows, right_rows):
    return lax.dot_general(
        left_rows,
        right_rows,
        (((1,), (1,)), ((), ())),
        precision=lax.Precision.HIGHEST,
        preferred_element_type=jnp.float32,
    )


def plain(vectors_left, vectors_right, amplitudes):
    count_a, count_c, left_q = vectors_left.shape
    count_b, count_d, right_q = vectors_right.shape
    left_whole = lax.all_gather(vectors_left, "vd", axis=2, tiled=True)
    left_flat = left_whole.reshape(count_a * count_c, left_whole.shape[2])
    piece = lax.all_gather(vectors_right, "vc", axis=2, tiled=True)
    width = piece.shape[2]
    tile = contract(left_flat, piece.reshape(count_b * count_d, width))
    tile = tile.reshape(count_a, count_c, count_b, count_d)
    partial_sum = jnp.einsum("acbd,cdi->iab", tile, amplitudes, precision=lax.Precision.HIGHEST)
    reduced = lax.psum_scatter(partial_sum, "vd", scatter_dimension=0, tiled=True)
    return lax.psum_scatter(reduced, "vc", scatter_dimension=2, tiled=True)


def split(x):
    hi = x.astype(jnp.bfloat16)
    lo = (x - hi.astype(jnp.float32)).astype(jnp.bfloat16)
    return hi, lo


def kernel(nz, nd, main, left, right, amps, out, lg, rg, te, acc, far,
           lbuf, rbuf, ls, rs, tbuf, total, red_d, red_c,
           in_send, in_recv, m_send, m_recv, e_send, e_recv, le_send, le_recv, te_send, te_recv,
           lg_send, lg_recv, d_send, d_recv, c_send, c_recv, local, tsem, keep):
    count_a, count_c, left_q = left.shape
    count_d, count_b, right_q = right.shape
    per = right_q // CHUNK
    rest = count_d - main
    halves = left_q // CHUNK
    rows_main, rows_rest = main * count_b, rest * count_b
    i = lax.axis_index("vc")
    j = lax.axis_index("vd")
    core, x, y = j % 2, (j // 2) % 2, j // 4
    jx, jy, js = j + 2 - 4 * x, j + 4 - 8 * y, j + 1 - 2 * core
    jd = jx + 4 - 8 * y
    is_end = (i == 0) | (i == nz - 1)
    middle = jnp.logical_not(is_end)
    partner = jnp.where(i < nz // 2, 1 - i, 2 * nz - 3 - i)
    across = nz - 1 - i

    barrier = pltpu.get_barrier_semaphore()
    for step in range(1, nd):
        pl.semaphore_signal(barrier, inc=1, device_id=(i, (j + step) % nd), device_id_type=MESH)
    for step in range(1, nz):
        pl.semaphore_signal(barrier, inc=1, device_id=((i + step) % nz, j), device_id_type=MESH)
    pl.semaphore_wait(barrier, nd - 1 + nz - 1)

    def remote(src, dst, send, recv, who):
        return pltpu.make_async_remote_copy(
            src_ref=src, dst_ref=dst, send_sem=send, recv_sem=recv, device_id=who, device_id_type=MESH)

    def mine(k, start, size):
        cols = pl.ds(pl.multiple_of(k * CHUNK, CHUNK), CHUNK)
        return right.at[pl.ds(start, size), :, cols]

    def in_copy(n, own):
        dst = rg.at[jnp.where(n < per, i, jnp.where(n < 2 * per, across, nz - 1 - partner)), n % per, pl.ds(0, main)]
        return remote(mine(n, 0, main) if own else dst, dst, in_send.at[n], in_recv.at[n], (partner, j))

    def e_copy(k):
        return remote(mine(k, 0, count_d), rg.at[i, k], e_send.at[k], e_recv.at[k], (partner, j))

    def m_start(n):
        @pl.when(n < per)
        def _():
            remote(mine(n, 0, count_d), rg.at[i, n], m_send.at[n], m_recv.at[n], (across, j)).start()

        @pl.when(n >= per)
        def _():
            block = rg.at[partner, n % per]
            remote(block, block, m_send.at[n], m_recv.at[n], (across, j)).start()

    def m_copy(n):
        ref = rg.at[jnp.where(n < per, across, nz - 1 - partner), n % per]
        return remote(ref, ref, m_send.at[n], m_recv.at[n], (across, j))

    def le_copy(h):
        return remote(lg.at[0, j, h], lg.at[1, j, h],
                      le_send.at[h], le_recv.at[h], (partner, j))

    def te_copy():
        return remote(amps.at[:, pl.ds(main, rest), :], te, te_send, te_recv, (partner, j))

    def lg_copy(g, n):
        h0, h1 = pl.ds(0, halves // 2), pl.ds(halves // 2, halves // 2)
        src, to = (
            (lg.at[g, j], jx), (lg.at[g, j], jy), (lg.at[g, j], js),
            (lg.at[g, jx, h0], jy), (lg.at[g, jy, h1], jx),
            (lg.at[g, jx], js), (lg.at[g, jy], js), (lg.at[g, jd], js),
        )[n]
        return remote(src, src, lg_send.at[g, n], lg_recv.at[g, n], (i, to))

    def lg_first(g):
        for n in (0, 1, 2):
            lg_copy(g, n).start()

    def lg_second(g):
        for n in (0, 1):
            lg_copy(g, n).wait_recv()
        for n in (3, 4, 5, 6):
            lg_copy(g, n).start()

    def lg_third(g):
        for n in (3, 4):
            lg_copy(g, n).wait_recv()
        lg_copy(g, 7).start()

    def lg_last(g):
        for n in (2, 5, 6, 7):
            lg_copy(g, n).wait_recv()

    def load_left(g, block, k):
        chunk = block * per + k
        src = lg.at[g, chunk // halves, chunk % halves]
        return pltpu.make_async_copy(src, lbuf, local.at[0])

    def load_right(block, k, start, size):
        src = rg.at[block, k, pl.ds(start, size)]
        return pltpu.make_async_copy(src, rbuf.at[pl.ds(start, size)], local.at[1 if start == 0 else 2])

    def split_left():
        @pl.loop(0, count_a)
        def _(a):
            hi, lo = split(lbuf[a])
            cols = pl.ds(pl.multiple_of(a * count_c, count_c), count_c)
            ls[0:CHUNK, cols] = hi
            ls[CHUNK:2 * CHUNK, cols] = lo
            ls[2 * CHUNK:3 * CHUNK, cols] = hi

    def split_right(start, size):
        @pl.loop(start // 8, (start + size) // 8)
        def _(g):
            hi, lo = split(rbuf[pl.ds(g * 8, 8)].reshape(8 * count_b, CHUNK))
            rows = pl.ds(pl.multiple_of(g * 8 * count_b, 8 * count_b), 8 * count_b)
            rs[rows, 0:CHUNK] = hi
            rs[rows, CHUNK:2 * CHUNK] = hi
            rs[rows, 2 * CHUNK:3 * CHUNK] = lo

    def multiply(target, span):
        first, size, wide = span
        width = wide * count_c

        @pl.loop(0, count_a // wide)
        def _(a):
            cols = pl.ds(pl.multiple_of(a * width, width), width)
            target[0:size, cols] += jnp.dot(
                rs[pl.ds(first, size), :], ls[:, cols], preferred_element_type=jnp.float32)

    main_span = (0, rows_main, 2)
    whole_span = (0, rows_main + rows_rest, 2)
    far_span = (rows_main, rows_rest, 4)

    def run(first, last, where, g, parts, target, span):
        def loads(q):
            block, k = where(q)
            return [load_left(g, block, k)] + [load_right(block, k, *part) for part in parts]

        @pl.when(first < last)
        def _():
            for copy in loads(first):
                copy.start()

        def task(q, carry):
            for copy in loads(q):
                copy.wait()
            split_left()
            for part in parts:
                split_right(*part)

            @pl.when(q + 1 < last)
            def _():
                for copy in loads(q + 1):
                    copy.start()

            multiply(target, span)
            return carry

        lax.fori_loop(first, last, task, 0)

    def from_middle(n):
        return jnp.where(n < per, across, nz - 1 - partner), n % per

    def from_partner(n):
        return jnp.where(i == 0, 1 + n // per, nz - 2 - n // per), n % per

    def end_task(q):
        block, k = from_partner(q - per)
        return jnp.where(q < per, i, block), jnp.where(q < per, q, k)

    def middle_task(q):
        r = q - per - 3
        from_end = (r >= 0) & (r < 7) & (r % 2 == 0)
        n = jnp.where(r < 0, q - per, jnp.where(r < 7, 3 + r // 2, q - 2 * per))
        block, k = from_middle(n)
        block, k = jnp.where(from_end, partner, block), jnp.where(from_end, r // 2, k)
        return jnp.where(q < per, i, block), jnp.where(q < per, q, k)

    def far_task(q):
        block, k = from_middle(q - 2 * per)
        return jnp.where(q < per, i, jnp.where(q < 2 * per, partner, block)), jnp.where(q < 2 * per, q % per, k)

    @pl.when(is_end)
    def _():
        e_copy(0).start()

    @pl.when(middle)
    def _():
        for n in range(AHEAD):
            m_start(n)
        for n in range(per):
            in_copy(n, True).start()

    keep_right = [pltpu.make_async_copy(mine(k, 0, count_d), rg.at[i, k], keep.at[k]) for k in range(per)]
    for copy in keep_right:
        copy.start()

    for h in range(halves):
        take = pltpu.make_async_copy(left.at[:, :, pl.ds(h * CHUNK, CHUNK)], lbuf, local.at[0])
        take.start()
        take.wait()

        @pl.loop(0, count_a)
        def _(a):
            lbuf[a] = lbuf[a].T

        give = pltpu.make_async_copy(lbuf, lg.at[0, j, h], local.at[0])
        give.start()
        give.wait()

        @pl.when(is_end)
        def _(h=h):
            le_copy(h).start()

    lg_first(0)

    @pl.loop(0, count_a)
    def _(a):
        cols = pl.ds(pl.multiple_of(a * count_c, count_c), count_c)
        acc[:, cols] = jnp.zeros((rows_main + rows_rest, count_c), jnp.float32)
        far[:, cols] = jnp.zeros((rows_rest, count_c), jnp.float32)

    for copy in keep_right:
        copy.wait()

    @pl.when(is_end)
    def _():
        @pl.loop(0, (nz - 1) * per)
        def _(t):
            block, k = from_partner(t)
            ref = rg.at[block, k, pl.ds(0, main)]
            remote(ref, ref, in_send.at[t], in_recv.at[t], (partner, j)).wait_recv()

            @pl.when(t == 2)
            def _():
                e_copy(1).start()
                lg_second(0)

            @pl.when(t == 3)
            def _():
                lg_third(0)

            @pl.when(t == 4)
            def _():
                e_copy(2).start()
                lg_last(0)

            @pl.when(t == 5)
            def _():
                e_copy(3).start()

            @pl.when(t == 7)
            def _():
                te_copy().start()

            def last(t):
                return jnp.where(t < 4, 0, jnp.minimum(t + 5, 4 * t - 10))

            run(last(t - 1), last(t), end_task, 0, ((0, main),), acc, main_span)

    @pl.when(middle)
    def _():
        @pl.loop(0, 2 * per)
        def _(t):
            m_copy(t).wait_recv()
            in_copy(t + per, False).start()

            @pl.when(t + AHEAD < 2 * per)
            def _():
                m_copy(t).wait_send()

                @pl.when(t + AHEAD >= per)
                def _():
                    e_copy(t + AHEAD - per).wait_recv()

                m_start(t + AHEAD)

            @pl.when(t == 1)
            def _():
                lg_second(0)

            @pl.when(t == 2)
            def _():
                lg_third(0)
                for h in range(halves):
                    le_copy(h).wait_recv()
                lg_first(1)
                lg_last(0)

            @pl.when(t == 5)
            def _():
                lg_second(1)

            @pl.when(t == 6)
            def _():
                lg_third(1)

            def last(t):
                return jnp.where(t < 2, 0, jnp.minimum(3 * t - 1, 9 + t))

            run(last(t - 1), last(t), middle_task, 0, ((0, main), (main, rest)), acc, whole_span)

        lg_last(1)
        run(0, nz * per, far_task, 1, ((main, rest),), far, far_span)

    total[...] = jnp.zeros_like(total)

    def amplitude_pass(source, first, groups, totals):
        def fetch(g, slot):
            return pltpu.make_async_copy(
                source.at[:, pl.ds(pl.multiple_of(first + g * 8, 8), 8), :], tbuf.at[slot], tsem.at[slot])

        fetch(0, 0).start()

        @pl.loop(0, groups)
        def _(g):
            slot = g % 2

            @pl.when(g + 1 < groups)
            def _():
                fetch(g + 1, 1 - slot).start()

            fetch(g, slot).wait()
            flat = tbuf.at[slot].reshape(count_c * 8, tbuf.shape[-1])
            part = jnp.zeros(total.shape, jnp.float32)
            for d in range(8):
                t_hi, t_lo = split(flat[pl.ds(d, count_c, stride=8), :])
                rows = pl.ds(pl.multiple_of((g * 8 + d) * count_b, count_b), count_b)
                wide = totals[rows, :]
                tall = jnp.concatenate(
                    [wide[:, a * count_c:(a + 1) * count_c] for a in range(count_a)], axis=0)
                x_hi, x_lo = split(tall)
                part += jnp.dot(
                    jnp.concatenate([x_hi, x_hi, x_lo], axis=1),
                    jnp.concatenate([t_hi, t_lo, t_hi], axis=0),
                    preferred_element_type=jnp.float32)
            total[...] += part

    amplitude_pass(amps, 0, jnp.where(middle, count_d // 8, main // 8), acc)

    @pl.when(middle)
    def _():
        te_copy().wait_recv()
        amplitude_pass(te, 0, rest // 8, far)

    total[...] = total[...].T

    size = out.shape[0]

    def d_copy(step, src_rows, slot, who):
        return remote(total.at[pl.ds(pl.multiple_of(src_rows * size, size), size)], red_d.at[slot],
                      d_send.at[step], d_recv.at[step], (i, who))

    for step in range(1, nd):
        to = (j + step) % nd
        d_copy(step, to, step, to).start()
    red_d[0] = total[pl.ds(pl.multiple_of(j * size, size), size), :]
    for step in range(1, nd):
        d_copy(step, j, step, js).wait_recv()
    here = red_d[0]
    for step in range(1, nd):
        here = here + red_d[step]
    red_c[0] = here

    def c_copy(step):
        return remote(red_c.at[0], red_c.at[step], c_send.at[step], c_recv.at[step], ((i + step) % nz, j))

    for step in range(1, nz):
        c_copy(step).start()
    for step in range(1, nz):
        c_copy(step).wait_recv()
    for step in range(1, nz):
        here = here + red_c[step]
    out[...] = here

    for step in range(1, nz):
        c_copy(step).wait_send()
    for step in range(1, nd):
        d_copy(step, j, step, js).wait_send()
    for n in range(8):
        lg_copy(0, n).wait_send()

    @pl.when(middle)
    def _():
        for n in range(8):
            lg_copy(1, n).wait_send()
        for n in range(AHEAD):
            m_copy(2 * per - AHEAD + n).wait_send()
        for n in range((nz - 1) * per):
            in_copy(n, False).wait_send()

    @pl.when(is_end)
    def _():
        for h in range(halves):
            le_copy(h).wait_send()
        for k in range(per):
            e_copy(k).wait_send()
        te_copy().wait_send()


def shards(nz, nd, main, vectors_left, vectors_right, amplitudes):
    count_a, count_c, left_q = vectors_left.shape
    count_b, count_d, right_q = vectors_right.shape
    pairs = amplitudes.shape[2]
    rest = count_d - main
    per = right_q // CHUNK
    f32, bf16 = jnp.float32, jnp.bfloat16
    columns = count_a * count_c
    dma = pltpu.SemaphoreType.DMA
    hbm = pl.BlockSpec(memory_space=pl.ANY)
    results = pl.pallas_call(
        functools.partial(kernel, nz, nd, main),
        out_shape=[
            jax.ShapeDtypeStruct((pairs // nd, count_a * count_b), f32),
            jax.ShapeDtypeStruct((2, nd, left_q // CHUNK, count_a, CHUNK, count_c), f32),
            jax.ShapeDtypeStruct((nz, per, count_d, count_b, CHUNK), f32),
            jax.ShapeDtypeStruct((count_c, rest, pairs), f32),
        ],
        in_specs=[hbm] * 3,
        out_specs=[pl.BlockSpec(memory_space=pltpu.VMEM), hbm, hbm, hbm],
        scratch_shapes=[
            pltpu.VMEM((count_d * count_b, columns), f32),
            pltpu.VMEM((rest * count_b, columns), f32),
            pltpu.VMEM((count_a, CHUNK, count_c), f32),
            pltpu.VMEM((count_d, count_b, CHUNK), f32),
            pltpu.VMEM((3 * CHUNK, columns), bf16),
            pltpu.VMEM((count_d * count_b, 3 * CHUNK), bf16),
            pltpu.VMEM((2, count_c, 8, pairs), f32),
            pltpu.VMEM((count_a * count_b, pairs), f32),
            pltpu.VMEM((nd, pairs // nd, count_a * count_b), f32),
            pltpu.VMEM((nz, pairs // nd, count_a * count_b), f32),
            dma(((nz - 1) * per,)), dma(((nz - 1) * per,)),
            dma((2 * per,)), dma((2 * per,)),
            dma((per,)), dma((per,)),
            dma((2,)), dma((2,)),
            dma, dma,
            dma((2, 8)), dma((2, 8)),
            dma((nd,)), dma((nd,)),
            dma((nz,)), dma((nz,)),
            dma((3,)), dma((2,)), dma((per,)),
        ],
        compiler_params=pltpu.CompilerParams(
            collective_id=0, has_side_effects=True, vmem_limit_bytes=52 * 2**20),
        name="ladder",
    )(vectors_left, jnp.transpose(vectors_right, (1, 0, 2)), amplitudes)
    whole = results[0].reshape(pairs // nd, count_a, count_b)
    width = count_b // nz
    return lax.dynamic_slice_in_dim(whole, lax.axis_index("vc") * width, width, axis=2)


def solution(mesh):
    nz, nd = mesh.shape["vc"], mesh.shape["vd"]
    fits = nz == 4 and nd == 8
    body = functools.partial(shards, nz, nd, 104) if fits else plain
    return jax.shard_map(
        body,
        mesh=mesh,
        in_specs=(P(None, "vc", "vd"), P(None, "vd", "vc"), P("vc", "vd", None)),
        out_specs=P("vd", None, "vc"),
        check_vma=False,
    )
```
